32 devices in a mesh: ma: 8 (over z, x), pol: 4 (over y, core).
Axes of the slice: x: 2, y: 2, z: 4, core: 2. Of those that a mesh axis runs over, the one named last changes fastest.
Arguments:
- sky_coeffs: bfloat16 [64, 4096], P('ma'), may hold values from -6 to 6
- visibilities: bfloat16 [64, 512], P('ma', 'pol'), may hold values from -6 to 6
- beam_blocks: bfloat16 [64, 512, 4096], P('ma', 'pol'), may hold values from -0.09375 to 0.09375
- mode_counts: int32 [64], P('ma'), may hold values from 128 to 512, as said below
- order_table: int32 [64], replicated, may hold values from 0 to 2047, as said below
- band_limits: int32 [8, 2], replicated, may hold values from 0 to 2048, as said below
Outputs:
- gradient: float32 [64, 4096], P('ma', 'pol')
The draws below stay inside these ranges and needn't reach their ends.
Inputs may be any that keep to these rules, and one draw needn't show every extreme that they name: `mode_counts`: the number of leading modes kept for the order of that row; some row keeps all 512. `order_table`: all entries differ. `band_limits`: row j is (low, high) with high - low between 512 and 1024.
All inputs are finite; a program needn't handle non-finite values.
Results may differ from the reference program's by a relative error of at most 0.0023.
Values may be sent and summed in bfloat16 or wider, within the bound.
A program may use at most 192 MiB of HBM per device.

```python
import math
import jax
import jax.numpy as jnp
from jax import lax

L = 2048
KMAX = 512
J = 8
M = 64
CYCLES = 4096


def draw_mode_counts(key, part):
    key = jax.random.fold_in(key, 12)
    first_key, second_key = jax.random.split(key)
    counts = jax.random.randint(first_key, (M,), KMAX // 4, KMAX + 1)
    shuffle = jax.random.permutation(second_key, M)
    counts = counts.at[shuffle[0]].set(KMAX).at[shuffle[1]].set(KMAX // 4)
    return counts.astype(jnp.int32)


def draw_order_table(key, part):
    key = jax.random.fold_in(key, 11)
    first_key, second_key = jax.random.split(key)
    stride = L // M
    offsets = jax.random.randint(first_key, (M,), 0, stride)
    orders = jnp.arange(M, dtype=jnp.int32) * stride + offsets
    orders = orders.at[0].set(0).at[M - 1].set(L - 1)
    shuffle = jax.random.permutation(second_key, M)
    return orders[shuffle].astype(jnp.int32)


def draw_band_limits(key, part):
    key = jax.random.fold_in(key, 13)
    first_key, second_key = jax.random.split(key)
    lowest = jax.random.randint(first_key, (J,), 0, L // 2)
    spread = jax.random.randint(second_key, (J,), L // 4, L // 2 + 1)
    lowest = lowest.at[0].set(0).at[1].set(L // 2)
    spread = spread.at[1].set(L // 2)
    return jnp.stack([lowest, lowest + spread], axis=1).astype(jnp.int32)


def shard_levels(rng, dims, cuts, least, high):
    loudness, own = 1.0, jax.random.fold_in(rng, 6)
    for position, blocks in cuts:
        steps = jnp.exp(jax.random.uniform(jax.random.fold_in(own, position), (blocks,), jnp.float32, least / len(cuts), high / len(cuts)))
        loudness = loudness * jnp.repeat(steps, dims[position] // blocks).reshape([-1 if axis == position else 1 for axis in range(len(dims))])
    return loudness


def scatter_about(key, extent, scale, bound, cuts=(), kind=jnp.bfloat16):
    gain = shard_levels(key, extent, cuts, -0.22, 0.18) if cuts else 1.0
    result = jax.random.normal(key, extent, jnp.float32) * scale * gain
    return jnp.minimum(jnp.maximum(result, -bound), bound).astype(kind)


def setup_inputs(seed: int = 0) -> dict:
    seeds = jax.random.split(jax.random.key(seed), 7)
    sky_coeffs = scatter_about(seeds[0], (M, 2 * L), 1.0, 6.0, ((0, 8),))
    visibilities = scatter_about(seeds[1], (M, KMAX), 1.0, 6.0, ((0, 8), (1, 4)))
    beam_blocks = scatter_about(seeds[2], (M, KMAX, 2 * L), (2 * L) ** -0.5, 0.09375, ((0, 8), (1, 4)))
    mode_counts = draw_mode_counts(jax.random.fold_in(seeds[6], 71), 0)
    order_table = draw_order_table(jax.random.fold_in(seeds[6], 71), 0)
    band_limits = draw_band_limits(jax.random.fold_in(seeds[6], 71), 0)
    return {"sky_coeffs": sky_coeffs, "visibilities": visibilities, "beam_blocks": beam_blocks, "mode_counts": mode_counts, "order_table": order_table, "band_limits": band_limits}


smoothing = 0.1
prior_weight = 0.2

def lat_tables(cycle_start, cycle_count):
    cycles_all = 2 * L
    ell_index = jnp.arange(L, dtype=jnp.int32)[:, None]
    cycle_index = cycle_start + jnp.arange(cycle_count, dtype=jnp.int32)[None, :]
    phase_steps = jnp.mod((2 * ell_index + 1) * (2 * cycle_index + 1) - cycles_all, 8 * cycles_all)
    angle = jnp.pi * phase_steps.astype(jnp.float32) / (4.0 * cycles_all)
    amplitude = math.sqrt(2.0 / L)
    return ((amplitude * jnp.cos(angle)).astype(jnp.bfloat16), (amplitude * jnp.sin(angle)).astype(jnp.bfloat16))

def order_phases(orders):
    quarter = jnp.mod(orders, 4)
    cos_phase = (quarter == 0).astype(jnp.float32) - (quarter == 2).astype(jnp.float32)
    sin_phase = (quarter == 1).astype(jnp.float32) - (quarter == 3).astype(jnp.float32)
    return (cos_phase, sin_phase)

def fourier_rows(orders):
    pixel_index = jnp.arange(2 * L, dtype=jnp.int32)
    steps_mod = jnp.mod(orders[:, None] * pixel_index[None, :], 2 * L)
    angle = 2.0 * jnp.pi * steps_mod.astype(jnp.float32) / (2.0 * L)
    norm_factor = 1.0 / math.sqrt(orders.shape[0])
    stacked = jnp.stack([jnp.cos(angle), -jnp.sin(angle)], axis=1) * norm_factor
    return stacked.reshape(2 * orders.shape[0], 2 * L).astype(jnp.bfloat16)

def band_kernel(limits):
    ell_index = jnp.arange(L, dtype=jnp.int32)[None, :]
    low_edge = limits[:, 0:1]
    high_edge = limits[:, 1:2]
    fraction = (ell_index - low_edge).astype(jnp.float32) / (high_edge - low_edge).astype(jnp.float32)
    inside = (ell_index >= low_edge) & (ell_index <= high_edge)
    return jnp.where(inside, jnp.sin(jnp.pi * fraction) ** 2, 0.0)

def cycle_weights(cycle_start, cycle_count):
    cycle_index = cycle_start + jnp.arange(cycle_count, dtype=jnp.int32)
    return jnp.sin(jnp.pi * (2 * cycle_index + 1).astype(jnp.float32) / (4.0 * L))

def reference(sky_coeffs, visibilities, beam_blocks, mode_counts, order_table, band_limits):
    ell_index = jnp.arange(2 * L, dtype=jnp.int32) % L
    alive_mask = ell_index[None, :] >= order_table[:, None]
    masked_sky = jnp.where(alive_mask, sky_coeffs, jnp.zeros_like(sky_coeffs))
    mode_index = jnp.arange(KMAX, dtype=jnp.int32)

    def one_order(inputs):
        block_rows, row_sky, row_vis, row_count = inputs
        image = jnp.dot(block_rows, row_sky, preferred_element_type=jnp.float32)
        misfit = jnp.where(mode_index < row_count, image - row_vis.astype(jnp.float32), 0.0).astype(jnp.bfloat16)
        return jnp.dot(misfit, block_rows, preferred_element_type=jnp.float32)
    data_term = lax.map(one_order, (beam_blocks, masked_sky, visibilities, mode_counts)) * alive_mask
    kernel_rows = band_kernel(band_limits)
    cosine_table, sine_table = lat_tables(0, CYCLES)
    fourier_table = fourier_rows(order_table)
    cos_phase, sin_phase = order_phases(order_table)
    cos_cols = jnp.repeat(cos_phase, 2)[:, None]
    sin_cols = jnp.repeat(sin_phase, 2)[:, None]
    weights = cycle_weights(0, CYCLES)
    coeffs = masked_sky.reshape(M, 2, L).astype(jnp.float32)

    def one_scale(running, scale_index):
        kernel_row = kernel_rows[scale_index]
        scaled = (kernel_row[None, None, :] * coeffs).astype(jnp.bfloat16).reshape(2 * M, L)
        synth = cos_cols * jnp.dot(scaled, cosine_table, preferred_element_type=jnp.float32) - sin_cols * jnp.dot(scaled, sine_table, preferred_element_type=jnp.float32)
        synth_b = synth.astype(jnp.bfloat16)
        pixels = jnp.dot(synth_b.T, fourier_table, preferred_element_type=jnp.float32)
        slopes = (weights[:, None] * pixels / jnp.sqrt(pixels * pixels + smoothing * smoothing)).astype(jnp.bfloat16)
        cycle_b = jnp.dot(slopes, fourier_table.T, preferred_element_type=jnp.float32).astype(jnp.bfloat16)
        harmonic = cos_cols * jnp.dot(cycle_b.T, cosine_table.T, preferred_element_type=jnp.float32) - sin_cols * jnp.dot(cycle_b.T, sine_table.T, preferred_element_type=jnp.float32)
        return (running + kernel_row[None, :] * harmonic, None)
    prior_sum, _ = lax.scan(one_scale, jnp.zeros((2 * M, L), jnp.float32), jnp.arange(J, dtype=jnp.int32))
    prior_term = prior_sum.reshape(M, 2 * L) * alive_mask
    return data_term + prior_weight * prior_term
```

```python
import functools
import math

import jax
import jax.numpy as jnp
from jax import lax
from jax.experimental import pallas as pl
from jax.experimental.pallas import tpu as pltpu
from jax.sharding import PartitionSpec as P

L = 2048
J = 8
CYCLES = 2 * L
FINE_ELL = 32
PIX_FINE = 128
PIX_TILE = 512
MESH = pl.DeviceIdType.MESH

smoothing = 0.1
prior_weight = 0.2


def order_phases(orders):
    quarter = jnp.mod(orders, 4)
    cos_phase = (quarter == 0).astype(jnp.float32) - (quarter == 2).astype(jnp.float32)
    sin_phase = (quarter == 1).astype(jnp.float32) - (quarter == 3).astype(jnp.float32)
    return (cos_phase, sin_phase)


def band_kernel(limits):
    ell_index = jnp.arange(L, dtype=jnp.int32)[None, :]
    low_edge = limits[:, 0:1]
    high_edge = limits[:, 1:2]
    fraction = (ell_index - low_edge).astype(jnp.float32) / (high_edge - low_edge).astype(
        jnp.float32
    )
    inside = (ell_index >= low_edge) & (ell_index <= high_edge)
    return jnp.where(inside, jnp.sin(jnp.pi * fraction) ** 2, 0.0)


def cycle_weights(cycle_start, cycle_count):
    cycle_index = cycle_start + jnp.arange(cycle_count, dtype=jnp.int32)
    return jnp.sin(jnp.pi * (2 * cycle_index + 1).astype(jnp.float32) / (4.0 * L))


def turn(steps, period):
    angle = (2.0 * jnp.pi / period) * jnp.mod(steps, period).astype(jnp.float32)
    return jnp.cos(angle), jnp.sin(angle)


def gather_kernel(
    n, share, half_ref, sky_ref, alive_ref, vis_ref, count_ref, beam_ref, all_ref, data_ref,
    beam_buf, beam_sem, send1, recv1, send2, recv2,
):
    ma = lax.axis_index("ma")
    pol = lax.axis_index("pol")
    side = lax.rem(pol, 2)
    mate = pol + 1 - 2 * side
    local_m, modes, width = beam_buf.shape

    def beam_copy(i):
        return pltpu.make_async_copy(beam_ref.at[i], beam_buf.at[i], beam_sem.at[i])

    def peer_copy(d):
        return pltpu.make_async_remote_copy(
            src_ref=half_ref.at[side], dst_ref=all_ref.at[side, ma],
            send_sem=send1.at[d], recv_sem=recv1.at[d],
            device_id=(lax.rem(ma + d, n), pol), device_id_type=MESH,
        )

    def mate_copy(d):
        source = lax.rem(ma + n - d, n)
        return pltpu.make_async_remote_copy(
            src_ref=all_ref.at[side, source], dst_ref=all_ref.at[side, source],
            send_sem=send2.at[d], recv_sem=recv2.at[d],
            device_id=(ma, mate), device_id_type=MESH,
        )

    for i in range(local_m):
        beam_copy(i).start()

    barrier = pltpu.get_barrier_semaphore()

    @pl.loop(1, n)
    def _(d):
        pl.semaphore_signal(
            barrier, inc=1, device_id=(lax.rem(ma + d, n), pol), device_id_type=MESH
        )

    pl.semaphore_signal(barrier, inc=1, device_id=(ma, mate), device_id_type=MESH)
    pl.semaphore_wait(barrier, n)

    @pl.loop(1, n)
    def _(d):
        peer_copy(d).start()

    all_ref[0, ma] = half_ref[0]
    all_ref[1, ma] = half_ref[1]

    mode_index = pol * modes + lax.broadcasted_iota(jnp.int32, (modes, 1), 0)

    def one_order(i):
        beam_copy(i).wait()
        mine = lax.broadcasted_iota(jnp.int32, (local_m, 1), 0) == i
        total = jnp.zeros((modes, 128), jnp.float32)
        for t in range(0, width, 128):
            row = sky_ref[i, :, t : t + 128]
            total = total + beam_buf[i, :, t : t + 128].astype(jnp.float32) * row
        image = jnp.sum(total, axis=1, keepdims=True)
        misfit = jnp.where(mode_index < count_ref[i], image - vis_ref[i], 0.0)
        spread = jnp.broadcast_to(
            misfit.astype(jnp.bfloat16).astype(jnp.float32), (modes, 128)
        )
        for t in range(0, width, 128):
            column = jnp.sum(
                beam_buf[i, :, t : t + 128].astype(jnp.float32) * spread, axis=0, keepdims=True
            )
            b, o = t // share, t % share
            data_ref[b, :, o : o + 128] += jnp.where(mine, column, 0.0)

    data_ref[...] = jnp.zeros_like(data_ref)
    early = local_m // 2

    @pl.loop(0, early)
    def _(i):
        one_order(i)

    @pl.loop(1, n)
    def _(d):
        peer_copy(d).wait_recv()
        mate_copy(d).start()

    @pl.loop(early, local_m)
    def _(i):
        one_order(i)

    for b in range(width // share):
        data_ref[b] = data_ref[b] * alive_ref[:, b * share : (b + 1) * share]

    @pl.loop(1, n)
    def _(d):
        peer_copy(d).wait_send()
        mate_copy(d).wait_send()
        mate_copy(d).wait_recv()


def prior_kernel(
    n, local_m, share, sky_ref, kern_ref, cp_ref, sp_ref, order_ref, weight_ref,
    lat_fc, lat_fs, lat_cc, lat_cs, four_fc, four_fs, four_cc, four_cs,
    fort_fc, fort_fs, fort_cc, fort_cs, out_ref,
    tab, four, fort, scaled, synth, total,
):
    scales = kern_ref.shape[0]
    rows = four.shape[0]
    cycles = tab.shape[1]
    amplitude = math.sqrt(2.0 / L)
    norm = 1.0 / math.sqrt(rows // 2)

    @pl.loop(0, tab.shape[0] // FINE_ELL)
    def _(b):
        cc = lat_cc[b] * amplitude
        cs = lat_cs[b] * amplitude
        at = pl.ds(pl.multiple_of(b * FINE_ELL, FINE_ELL), FINE_ELL)
        tab[at, :] = (lat_fc[...] * cc - lat_fs[...] * cs).astype(jnp.bfloat16)

    for b in range(CYCLES // PIX_FINE):
        at = slice(b * PIX_FINE, (b + 1) * PIX_FINE)
        four[:, at] = (
            (four_fc[...] * four_cc[:, b : b + 1] - four_fs[...] * four_cs[:, b : b + 1]) * norm
        ).astype(jnp.bfloat16)
        fort[at, :] = (
            (fort_fc[...] * fort_cc[b : b + 1, :] - fort_fs[...] * fort_cs[b : b + 1, :]) * norm
        ).astype(jnp.bfloat16)

    half = L // 2
    for j in range(scales):
        for h in range(2):
            scaled[j * rows : (j + 1) * rows, h * half : (h + 1) * half] = (
                kern_ref[j : j + 1, h * half : (h + 1) * half] * sky_ref[h].astype(jnp.float32)
            ).astype(jnp.bfloat16)
    for j in range(scales):
        part = scaled[j * rows : (j + 1) * rows, :]
        with_cos = jnp.dot(part, tab[0:L, :], preferred_element_type=jnp.float32)
        with_sin = jnp.dot(part, tab[L : 2 * L, :], preferred_element_type=jnp.float32)
        synth[j * rows : (j + 1) * rows, :] = (
            cp_ref[...] * with_cos - sp_ref[...] * with_sin
        ).astype(jnp.bfloat16)

    total[...] = jnp.zeros_like(total)

    @pl.loop(0, CYCLES // PIX_TILE)
    def _(t):
        at = pl.ds(pl.multiple_of(t * PIX_TILE, PIX_TILE), PIX_TILE)
        left = fort[at, :]
        right = four[:, at]
        for j in range(scales):
            mine = slice(j * rows, (j + 1) * rows)
            pixels = jnp.dot(left, synth[mine, :], preferred_element_type=jnp.float32)
            slopes = (
                weight_ref[...] * pixels * lax.rsqrt(pixels * pixels + smoothing * smoothing)
            ).astype(jnp.bfloat16)
            total[mine, :] += jnp.dot(right, slopes, preferred_element_type=jnp.float32)

    contract_last = (((1,), (1,)), ((), ()))
    for t in range(0, L, share):
        ell = t + lax.broadcasted_iota(jnp.int32, (1, share), 1)
        prior = jnp.zeros((rows, share), jnp.float32)
        for j in range(scales):
            cycle_b = total[j * rows : (j + 1) * rows, :].astype(jnp.bfloat16)
            back_cos = lax.dot_general(
                cycle_b, tab[t : t + share, :], contract_last, preferred_element_type=jnp.float32
            )
            back_sin = lax.dot_general(
                cycle_b, tab[L + t : L + t + share, :], contract_last,
                preferred_element_type=jnp.float32,
            )
            prior = prior + kern_ref[j : j + 1, t : t + share] * (
                cp_ref[...] * back_cos - sp_ref[...] * back_sin
            )
        prior = jnp.where(ell >= order_ref[...], prior_weight * prior, 0.0)
        for d in range(n):
            for c in range(2):
                first = (2 * d + c) * local_m
                piece = prior[first : first + local_m, :]
                out_ref[(c * L + t) // share, d] = jnp.concatenate(
                    [piece[:, : share // 2], piece[:, share // 2 :]], axis=0
                ).astype(jnp.bfloat16)


def reduce_kernel(
    n, pols, prior_ref, data_ref, out_ref, mate_in, sums, peer_in, data_in,
    send_a, recv_a, send_b, recv_b, send_d, recv_d,
):
    ma = lax.axis_index("ma")
    pol = lax.axis_index("pol")
    side = lax.rem(pol, 2)
    mate = pol + 1 - 2 * side
    pairs = pols // 2
    pair = pol // 2
    everyone = n * pairs
    place = ma * pairs + pair
    local_m = out_ref.shape[0]
    share = out_ref.shape[1]

    def data_copy(d):
        other = lax.rem(pol + d, pols)
        return pltpu.make_async_remote_copy(
            src_ref=data_ref.at[other], dst_ref=data_in.at[d - 1],
            send_sem=send_d.at[d - 1], recv_sem=recv_d.at[d - 1],
            device_id=(ma, other), device_id_type=MESH,
        )

    def mate_copy(h):
        return pltpu.make_async_remote_copy(
            src_ref=prior_ref.at[2 * h + 1 - side], dst_ref=mate_in.at[h],
            send_sem=send_a.at[h], recv_sem=recv_a.at[h],
            device_id=(ma, mate), device_id_type=MESH,
        )

    def peer_copy(d):
        target = lax.rem(place + d, everyone)
        target_ma = target // pairs
        target_pair = lax.rem(target, pairs)
        return pltpu.make_async_remote_copy(
            src_ref=sums.at[target_pair, target_ma], dst_ref=peer_in.at[d - 1],
            send_sem=send_b.at[d - 1], recv_sem=recv_b.at[d - 1],
            device_id=(target_ma, 2 * target_pair + side), device_id_type=MESH,
        )

    barrier = pltpu.get_barrier_semaphore()

    @pl.loop(1, everyone)
    def _(d):
        target = lax.rem(place + d, everyone)
        pl.semaphore_signal(
            barrier, inc=1,
            device_id=(target // pairs, 2 * lax.rem(target, pairs) + side), device_id_type=MESH,
        )

    for d in range(1, pols, 2):
        pl.semaphore_signal(
            barrier, inc=1, device_id=(ma, lax.rem(pol + d, pols)), device_id_type=MESH
        )
    pl.semaphore_wait(barrier, everyone - 1 + pairs)

    for h in range(pairs):
        mate_copy(h).start()
    for d in range(1, pols):
        data_copy(d).start()
    for h in range(pairs):
        mate_copy(h).wait_recv()
        sums[h] = (
            prior_ref[2 * h + side].astype(jnp.float32) + mate_in[h].astype(jnp.float32)
        ).astype(jnp.bfloat16)

    @pl.loop(1, everyone)
    def _(d):
        peer_copy(d).start()

    result = data_ref[pol]
    for d in range(1, pols):
        data_copy(d).wait_recv()
        result = result + data_in[d - 1]

    def add(d, running):
        peer_copy(d).wait_recv()
        return running + peer_in[d - 1].astype(jnp.float32)

    prior = lax.fori_loop(1, everyone, add, sums[pair, ma].astype(jnp.float32))
    out_ref[:, : share // 2] = result[:, : share // 2] + prior[:local_m]
    out_ref[:, share // 2 :] = result[:, share // 2 :] + prior[local_m:]

    for h in range(pairs):
        mate_copy(h).wait_send()
    for d in range(1, pols):
        data_copy(d).wait_send()

    @pl.loop(1, everyone)
    def _(d):
        peer_copy(d).wait_send()


def shards(sky_coeffs, visibilities, beam_blocks, mode_counts, order_table, band_limits):
    local_m, width = sky_coeffs.shape
    modes = beam_blocks.shape[1]
    n = lax.axis_size("ma")
    pols = lax.axis_size("pol")
    ma_pos = lax.axis_index("ma")
    pol_pos = lax.axis_index("pol")
    cycles = CYCLES // n
    scales = J // pols
    share = width // pols
    rows = 2 * n * local_m
    vmem = pl.BlockSpec(memory_space=pltpu.VMEM)
    smem = pl.BlockSpec(memory_space=pltpu.SMEM)
    hbm = pl.BlockSpec(memory_space=pl.ANY)
    f32, bf16, i32 = jnp.float32, jnp.bfloat16, jnp.int32
    shape = jax.ShapeDtypeStruct
    sem = pltpu.SemaphoreType.DMA

    local_orders = lax.dynamic_slice_in_dim(order_table, ma_pos * local_m, local_m)
    ell_index = jnp.arange(width, dtype=i32) % L
    alive = ell_index[None, :] >= local_orders[:, None]
    masked = jnp.where(alive, sky_coeffs, jnp.zeros_like(sky_coeffs))
    halves = masked.reshape(local_m, 2, 2, L // 2).transpose(2, 1, 0, 3)
    halves = halves.reshape(2, 2 * local_m, L // 2)
    everything, data = pl.pallas_call(
        functools.partial(gather_kernel, n, share),
        out_shape=(
            shape((2, n, 2 * local_m, L // 2), bf16), shape((pols, local_m, share), f32),
        ),
        in_specs=[vmem, vmem, vmem, vmem, smem, hbm],
        out_specs=(vmem, vmem),
        scratch_shapes=[
            pltpu.VMEM((local_m, modes, width), bf16), sem((local_m,)),
            sem((n,)), sem((n,)), sem((n,)), sem((n,)),
        ],
        compiler_params=pltpu.CompilerParams(
            collective_id=0, has_side_effects=True, vmem_limit_bytes=40 * 2**20
        ),
    )(
        halves, masked.astype(f32)[:, None, :], alive.astype(f32), visibilities.astype(f32)[:, :, None],
        mode_counts, beam_blocks,
    )

    my_limits = lax.dynamic_slice_in_dim(band_limits, pol_pos * scales, scales, 0)
    kernel_rows = band_kernel(my_limits)
    row_orders = jnp.broadcast_to(order_table.reshape(n, 1, local_m), (n, 2, local_m)).reshape(rows)
    row_part = jnp.broadcast_to(
        jnp.arange(2, dtype=i32)[None, :, None], (n, 2, local_m)
    ).reshape(rows)
    cos_phase, sin_phase = order_phases(row_orders)
    weights = cycle_weights(ma_pos * cycles, cycles)
    period = 8 * CYCLES
    cycle_odd = 2 * (ma_pos * cycles + jnp.arange(cycles, dtype=i32))[None, :] + 1
    fine = 2 * jnp.arange(FINE_ELL, dtype=i32)[:, None] + 1
    coarse = 2 * FINE_ELL * jnp.arange(L // FINE_ELL, dtype=i32)[:, None]
    coarse_steps = coarse * cycle_odd - CYCLES
    lat_fine = turn(fine * cycle_odd, period)
    lat_coarse = turn(jnp.concatenate([coarse_steps, coarse_steps - period // 4]), period)
    lat_coarse = [table[:, None, :] for table in lat_coarse]
    pix_fine = jnp.arange(PIX_FINE, dtype=i32)
    pix_coarse = PIX_FINE * jnp.arange(CYCLES // PIX_FINE, dtype=i32)
    four_fine = turn(row_orders[:, None] * pix_fine[None, :], CYCLES)
    four_coarse = turn(
        row_orders[:, None] * pix_coarse[None, :] + (CYCLES // 4) * row_part[:, None], CYCLES
    )
    fort_fine = turn(row_orders[None, :] * pix_fine[:, None], CYCLES)
    fort_coarse = turn(
        row_orders[None, :] * pix_coarse[:, None] + (CYCLES // 4) * row_part[None, :], CYCLES
    )
    prior = pl.pallas_call(
        functools.partial(prior_kernel, n, local_m, share),
        out_shape=shape((pols, n, 2 * local_m, share // 2), bf16),
        in_specs=[vmem] * 18,
        out_specs=vmem,
        scratch_shapes=[
            pltpu.VMEM((2 * L, cycles), bf16),
            pltpu.VMEM((rows, CYCLES), bf16),
            pltpu.VMEM((CYCLES, rows), bf16),
            pltpu.VMEM((scales * rows, L), bf16),
            pltpu.VMEM((scales * rows, cycles), bf16),
            pltpu.VMEM((scales * rows, cycles), f32),
        ],
        compiler_params=pltpu.CompilerParams(vmem_limit_bytes=56 * 2**20),
    )(
        everything.reshape(2, rows, L // 2), kernel_rows, cos_phase[:, None], sin_phase[:, None],
        row_orders[:, None], weights[None, :],
        *lat_fine, *lat_coarse, *four_fine, *four_coarse, *fort_fine, *fort_coarse,
    )

    everyone = n * (pols // 2)
    piece = (2 * local_m, share // 2)
    return pl.pallas_call(
        functools.partial(reduce_kernel, n, pols),
        out_shape=shape((local_m, share), f32),
        in_specs=[vmem, vmem],
        out_specs=vmem,
        scratch_shapes=[
            pltpu.VMEM((pols // 2, n) + piece, bf16),
            pltpu.VMEM((pols // 2, n) + piece, bf16),
            pltpu.VMEM((everyone - 1,) + piece, bf16),
            pltpu.VMEM((pols - 1, local_m, share), f32),
            sem((pols // 2,)), sem((pols // 2,)),
            sem((everyone - 1,)), sem((everyone - 1,)),
            sem((pols - 1,)), sem((pols - 1,)),
        ],
        compiler_params=pltpu.CompilerParams(
            collective_id=1, has_side_effects=True, vmem_limit_bytes=40 * 2**20
        ),
    )(prior, data)


def solution(mesh):
    placed = (P("ma", None), P("ma", "pol"), P("ma", "pol", None), P("ma"), P(), P())
    return jax.shard_map(
        shards, mesh=mesh, in_specs=placed, out_specs=P("ma", "pol"), check_vma=False
    )
```

```python
import functools
import math

import jax
import jax.numpy as jnp
from jax import lax
from jax.experimental import pallas as pl
from jax.experimental.pallas import tpu as pltpu
from jax.sharding import PartitionSpec as P

L = 2048
J = 8
CYCLES = 2 * L
FINE_ELL = 32
PIX_FINE = 128
PIX_TILE = 512
MESH = pl.DeviceIdType.MESH

smoothing = 0.1
prior_weight = 0.2


def short_waves(angle):
    z = angle * angle
    sine = angle * (1.0 + z * (-1.0 / 6 + z * (1.0 / 120 + z * (-1.0 / 5040 + z / 362880.0))))
    cosine = 1.0 + z * (
        -0.5 + z * (1.0 / 24 + z * (-1.0 / 720 + z * (1.0 / 40320 - z / 3628800.0)))
    )
    return cosine, sine


def turn(steps, period):
    centred = jnp.bitwise_and(steps, period - 1) - period // 2
    cosine, sine = short_waves(centred.astype(jnp.float32) * (0.5 * math.pi / period))
    cosine, sine = 1.0 - 2.0 * sine * sine, 2.0 * sine * cosine
    return 2.0 * sine * sine - 1.0, -2.0 * sine * cosine


def band_row(low, high):
    ell = lax.broadcasted_iota(jnp.int32, (1, L), 1)
    span = jnp.full((1, L), high - low, jnp.int32).astype(jnp.float32)
    fraction = (ell - low).astype(jnp.float32) / span
    inside = (ell >= low) & (ell <= high)
    cosine, sine = short_waves(0.5 * math.pi * (jnp.where(inside, fraction, 0.5) - 0.5))
    return jnp.where(inside, (1.0 - 2.0 * sine * sine) ** 2, 0.0)


def gather_kernel(
    n, share, sky_ref, order_ref, vis_ref, count_ref, beam_ref, all_ref, data_ref,
    sky_rows, vis_rows, beam_buf, beam_sem, send1, recv1, send2, recv2,
):
    ma = lax.axis_index("ma")
    pol = lax.axis_index("pol")
    side = lax.rem(pol, 2)
    mate = pol + 1 - 2 * side
    local_m, modes, width = beam_buf.shape

    def beam_copy(i):
        return pltpu.make_async_copy(beam_ref.at[i], beam_buf.at[i], beam_sem.at[i])

    def peer_copy(d):
        return pltpu.make_async_remote_copy(
            src_ref=all_ref.at[side, ma], dst_ref=all_ref.at[side, ma],
            send_sem=send1.at[d], recv_sem=recv1.at[d],
            device_id=(lax.rem(ma + d, n), pol), device_id_type=MESH,
        )

    def mate_copy(d):
        source = lax.rem(ma + n - d, n)
        return pltpu.make_async_remote_copy(
            src_ref=all_ref.at[side, source], dst_ref=all_ref.at[side, source],
            send_sem=send2.at[d], recv_sem=recv2.at[d],
            device_id=(ma, mate), device_id_type=MESH,
        )

    for i in range(local_m):
        beam_copy(i).start()

    orders = order_ref[pl.ds(pl.multiple_of(ma * local_m, local_m), local_m), :]
    alive = lax.rem(lax.broadcasted_iota(jnp.int32, (1, width), 1), L) >= orders
    masked = jnp.where(alive, sky_ref[...].astype(jnp.float32), 0.0)
    half = L // 2
    for h in range(2):
        all_ref[h, ma] = jnp.concatenate(
            [masked[:, h * half : (h + 1) * half], masked[:, L + h * half : L + (h + 1) * half]],
            axis=0,
        ).astype(jnp.bfloat16)
    vis = vis_ref[...].astype(jnp.float32)
    for i in range(local_m):
        sky_rows[i] = masked[i : i + 1]
        vis_rows[i] = vis[i : i + 1]

    barrier = pltpu.get_barrier_semaphore()

    @pl.loop(1, n)
    def _(d):
        pl.semaphore_signal(
            barrier, inc=1, device_id=(lax.rem(ma + d, n), pol), device_id_type=MESH
        )

    pl.semaphore_signal(barrier, inc=1, device_id=(ma, mate), device_id_type=MESH)
    pl.semaphore_wait(barrier, n)

    @pl.loop(1, n)
    def _(d):
        peer_copy(d).start()

    mode_index = pol * modes + lax.broadcasted_iota(jnp.int32, (modes, 1), 0)
    diagonal = lax.broadcasted_iota(jnp.int32, (modes, modes), 0) == lax.broadcasted_iota(
        jnp.int32, (modes, modes), 1
    )

    def one_order(i):
        beam_copy(i).wait()
        mine = lax.broadcasted_iota(jnp.int32, (local_m, 1), 0) == i
        total = jnp.where(diagonal, -vis_rows[i], 0.0)
        for t in range(0, width, 128):
            row = sky_rows[i, :, t : t + 128]
            total = total + beam_buf[i, :, t : t + 128].astype(jnp.float32) * row
        image = jnp.sum(total, axis=1, keepdims=True)
        misfit = jnp.where(mode_index < count_ref[i], image, 0.0)
        spread = jnp.broadcast_to(
            misfit.astype(jnp.bfloat16).astype(jnp.float32), (modes, 128)
        )
        for t in range(0, width, 128):
            column = jnp.sum(
                beam_buf[i, :, t : t + 128].astype(jnp.float32) * spread, axis=0, keepdims=True
            )
            b, o = t // share, t % share
            data_ref[b, :, o : o + 128] += jnp.where(mine, column, 0.0)

    data_ref[...] = jnp.zeros_like(data_ref)
    early = local_m // 2

    @pl.loop(0, early)
    def _(i):
        one_order(i)

    @pl.loop(1, n)
    def _(d):
        peer_copy(d).wait_recv()
        mate_copy(d).start()

    @pl.loop(early, local_m)
    def _(i):
        one_order(i)

    for b in range(width // share):
        ell = lax.rem(b * share + lax.broadcasted_iota(jnp.int32, (1, share), 1), L)
        data_ref[b] = jnp.where(ell >= orders, data_ref[b], 0.0)

    @pl.loop(1, n)
    def _(d):
        peer_copy(d).wait_send()
        mate_copy(d).wait_send()
        mate_copy(d).wait_recv()


def prior_kernel(
    n, local_m, share, sky_ref, limit_ref, order_ref, turned_ref, out_ref,
    tab, four, fort, coarse_cos, coarse_sin, scaled, synth, total,
):
    ma = lax.axis_index("ma")
    pol = lax.axis_index("pol")
    rows = four.shape[0]
    cycles = tab.shape[1]
    scales = synth.shape[0] // rows
    amplitude = math.sqrt(2.0 / L)
    norm = 1.0 / math.sqrt(rows // 2)

    def index(count, axis):
        return lax.broadcasted_iota(jnp.int32, (count, 1) if axis == 0 else (1, count), axis)

    kern = [
        band_row(limit_ref[pol * scales + j, 0], limit_ref[pol * scales + j, 1])
        for j in range(scales)
    ]
    quarter = jnp.bitwise_and(order_ref[...], 3)
    cp = jnp.where(quarter == 0, 1.0, jnp.where(quarter == 2, -1.0, 0.0))
    sp = jnp.where(quarter == 1, 1.0, jnp.where(quarter == 3, -1.0, 0.0))
    odd = 2 * (ma * cycles + index(cycles, 1)) + 1
    _, weight = turn(odd, 4 * CYCLES)

    period = 8 * CYCLES
    blocks = L // FINE_ELL
    coarse = 2 * FINE_ELL * index(blocks, 0) * odd - CYCLES
    for part in range(2):
        cosine, sine = turn(coarse - part * (period // 4), period)
        for b in range(blocks):
            coarse_cos[part * blocks + b] = amplitude * cosine[b : b + 1]
            coarse_sin[part * blocks + b] = amplitude * sine[b : b + 1]
    fine_cos, fine_sin = turn((2 * index(FINE_ELL, 0) + 1) * odd, period)

    @pl.loop(0, 2 * blocks)
    def _(b):
        at = pl.ds(pl.multiple_of(b * FINE_ELL, FINE_ELL), FINE_ELL)
        tab[at, :] = (fine_cos * coarse_cos[b] - fine_sin * coarse_sin[b]).astype(jnp.bfloat16)

    steps = CYCLES // PIX_FINE
    down, across = order_ref[...], turned_ref[...]
    quarter_turn = CYCLES // 4
    down_part = lax.rem(index(rows, 0) // local_m, 2) * quarter_turn
    across_part = lax.rem(index(rows, 1) // local_m, 2) * quarter_turn
    down_fine = turn(down * index(PIX_FINE, 1), CYCLES)
    down_coarse = turn(down * (PIX_FINE * index(steps, 1)) + down_part, CYCLES)
    across_fine = turn(across * index(PIX_FINE, 0), CYCLES)
    across_coarse = turn(across * (PIX_FINE * index(steps, 0)) + across_part, CYCLES)
    down_fine = [norm * part for part in down_fine]
    across_fine = [norm * part for part in across_fine]
    for b in range(steps):
        at = slice(b * PIX_FINE, (b + 1) * PIX_FINE)
        four[:, at] = (
            down_fine[0] * down_coarse[0][:, b : b + 1]
            - down_fine[1] * down_coarse[1][:, b : b + 1]
        ).astype(jnp.bfloat16)
        fort[at, :] = (
            across_fine[0] * across_coarse[0][b : b + 1, :]
            - across_fine[1] * across_coarse[1][b : b + 1, :]
        ).astype(jnp.bfloat16)

    half = L // 2
    for j in range(scales):
        for h in range(2):
            scaled[j * rows : (j + 1) * rows, h * half : (h + 1) * half] = (
                kern[j][:, h * half : (h + 1) * half] * sky_ref[h].astype(jnp.float32)
            ).astype(jnp.bfloat16)
    for j in range(scales):
        part = scaled[j * rows : (j + 1) * rows, :]
        with_cos = jnp.dot(part, tab[0:L, :], preferred_element_type=jnp.float32)
        with_sin = jnp.dot(part, tab[L : 2 * L, :], preferred_element_type=jnp.float32)
        synth[j * rows : (j + 1) * rows, :] = (
            cp * with_cos - sp * with_sin
        ).astype(jnp.bfloat16)

    total[...] = jnp.zeros_like(total)

    @pl.loop(0, CYCLES // PIX_TILE)
    def _(t):
        at = pl.ds(pl.multiple_of(t * PIX_TILE, PIX_TILE), PIX_TILE)
        left = fort[at, :]
        right = four[:, at]
        for j in range(scales):
            mine = slice(j * rows, (j + 1) * rows)
            pixels = jnp.dot(left, synth[mine, :], preferred_element_type=jnp.float32)
            slopes = (
                weight * pixels * lax.rsqrt(pixels * pixels + smoothing * smoothing)
            ).astype(jnp.bfloat16)
            total[mine, :] += jnp.dot(right, slopes, preferred_element_type=jnp.float32)

    contract_last = (((1,), (1,)), ((), ()))
    for t in range(0, L, share):
        ell = t + lax.broadcasted_iota(jnp.int32, (1, share), 1)
        prior = jnp.zeros((rows, share), jnp.float32)
        for j in range(scales):
            cycle_b = total[j * rows : (j + 1) * rows, :].astype(jnp.bfloat16)
            back_cos = lax.dot_general(
                cycle_b, tab[t : t + share, :], contract_last, preferred_element_type=jnp.float32
            )
            back_sin = lax.dot_general(
                cycle_b, tab[L + t : L + t + share, :], contract_last,
                preferred_element_type=jnp.float32,
            )
            prior = prior + kern[j][:, t : t + share] * (
                cp * back_cos - sp * back_sin
            )
        prior = jnp.where(ell >= order_ref[...], prior_weight * prior, 0.0)
        for d in range(n):
            for c in range(2):
                first = (2 * d + c) * local_m
                piece = prior[first : first + local_m, :]
                out_ref[(c * L + t) // share, d] = piece


def reduce_kernel(
    n, pols, prior_ref, data_ref, out_ref, mate_in, sums, peer_in, data_in,
    send_a, recv_a, send_b, recv_b, send_d, recv_d,
):
    ma = lax.axis_index("ma")
    pol = lax.axis_index("pol")
    side = lax.rem(pol, 2)
    mate = pol + 1 - 2 * side
    pairs = pols // 2
    pair = pol // 2
    everyone = n * pairs
    place = ma * pairs + pair
    local_m = out_ref.shape[0]
    share = out_ref.shape[1]

    def data_copy(d):
        other = lax.rem(pol + d, pols)
        return pltpu.make_async_remote_copy(
            src_ref=data_ref.at[other], dst_ref=data_in.at[d - 1],
            send_sem=send_d.at[d - 1], recv_sem=recv_d.at[d - 1],
            device_id=(ma, other), device_id_type=MESH,
        )

    def mate_copy(h):
        return pltpu.make_async_remote_copy(
            src_ref=prior_ref.at[2 * h + 1 - side], dst_ref=mate_in.at[h],
            send_sem=send_a.at[h], recv_sem=recv_a.at[h],
            device_id=(ma, mate), device_id_type=MESH,
        )

    def peer_copy(d):
        target = lax.rem(place + d, everyone)
        target_ma = target // pairs
        target_pair = lax.rem(target, pairs)
        return pltpu.make_async_remote_copy(
            src_ref=sums.at[target_pair, target_ma], dst_ref=peer_in.at[d - 1],
            send_sem=send_b.at[d - 1], recv_sem=recv_b.at[d - 1],
            device_id=(target_ma, 2 * target_pair + side), device_id_type=MESH,
        )

    barrier = pltpu.get_barrier_semaphore()

    @pl.loop(1, everyone)
    def _(d):
        target = lax.rem(place + d, everyone)
        pl.semaphore_signal(
            barrier, inc=1,
            device_id=(target // pairs, 2 * lax.rem(target, pairs) + side), device_id_type=MESH,
        )

    for d in range(1, pols, 2):
        pl.semaphore_signal(
            barrier, inc=1, device_id=(ma, lax.rem(pol + d, pols)), device_id_type=MESH
        )
    pl.semaphore_wait(barrier, everyone - 1 + pairs)

    for h in range(pairs):
        mate_copy(h).start()
    for d in range(1, pols):
        data_copy(d).start()
    for h in range(pairs):
        mate_copy(h).wait_recv()
        both = prior_ref[2 * h + side] + mate_in[h]
        sums[h] = jnp.concatenate(
            [both[:, :, : share // 2], both[:, :, share // 2 :]], axis=1
        ).astype(jnp.bfloat16)

    @pl.loop(1, everyone)
    def _(d):
        peer_copy(d).start()

    result = data_ref[pol] + (prior_ref[pol, ma] + mate_in[pair, ma])
    for d in range(1, pols):
        data_copy(d).wait_recv()
        result = result + data_in[d - 1]

    def add(d, running):
        peer_copy(d).wait_recv()
        return running + peer_in[d - 1].astype(jnp.float32)

    prior = lax.fori_loop(1, everyone, add, jnp.zeros(peer_in.shape[1:], jnp.float32))
    out_ref[:, : share // 2] = result[:, : share // 2] + prior[:local_m]
    out_ref[:, share // 2 :] = result[:, share // 2 :] + prior[local_m:]

    for h in range(pairs):
        mate_copy(h).wait_send()
    for d in range(1, pols):
        data_copy(d).wait_send()

    @pl.loop(1, everyone)
    def _(d):
        peer_copy(d).wait_send()


def shards(sky_coeffs, visibilities, beam_blocks, mode_counts, order_table, band_limits):
    local_m, width = sky_coeffs.shape
    modes = beam_blocks.shape[1]
    n = lax.axis_size("ma")
    pols = lax.axis_size("pol")
    cycles = CYCLES // n
    scales = J // pols
    share = width // pols
    rows = 2 * n * local_m
    vmem = pl.BlockSpec(memory_space=pltpu.VMEM)
    smem = pl.BlockSpec(memory_space=pltpu.SMEM)
    hbm = pl.BlockSpec(memory_space=pl.ANY)
    f32, bf16 = jnp.float32, jnp.bfloat16
    shape = jax.ShapeDtypeStruct
    sem = pltpu.SemaphoreType.DMA

    everything, data = pl.pallas_call(
        functools.partial(gather_kernel, n, share),
        out_shape=(
            shape((2, n, 2 * local_m, L // 2), bf16), shape((pols, local_m, share), f32),
        ),
        in_specs=[vmem, vmem, vmem, smem, hbm],
        out_specs=(vmem, vmem),
        scratch_shapes=[
            pltpu.VMEM((local_m, 1, width), f32), pltpu.VMEM((local_m, 1, modes), f32),
            pltpu.VMEM((local_m, modes, width), bf16), sem((local_m,)),
            sem((n,)), sem((n,)), sem((n,)), sem((n,)),
        ],
        compiler_params=pltpu.CompilerParams(
            collective_id=0, has_side_effects=True, vmem_limit_bytes=40 * 2**20
        ),
    )(
        sky_coeffs, order_table[:, None], visibilities, mode_counts, beam_blocks
    )

    row_orders = jnp.broadcast_to(order_table.reshape(n, 1, local_m), (n, 2, local_m)).reshape(rows)
    prior = pl.pallas_call(
        functools.partial(prior_kernel, n, local_m, share),
        out_shape=shape((pols, n, local_m, share), f32),
        in_specs=[vmem, smem, vmem, vmem],
        out_specs=vmem,
        scratch_shapes=[
            pltpu.VMEM((2 * L, cycles), bf16),
            pltpu.VMEM((rows, CYCLES), bf16),
            pltpu.VMEM((CYCLES, rows), bf16),
            pltpu.VMEM((2 * L // FINE_ELL, 1, cycles), f32),
            pltpu.VMEM((2 * L // FINE_ELL, 1, cycles), f32),
            pltpu.VMEM((scales * rows, L), bf16),
            pltpu.VMEM((scales * rows, cycles), bf16),
            pltpu.VMEM((scales * rows, cycles), f32),
        ],
        compiler_params=pltpu.CompilerParams(vmem_limit_bytes=56 * 2**20),
    )(
        everything.reshape(2, rows, L // 2), band_limits, row_orders[:, None], row_orders[None, :]
    )

    everyone = n * (pols // 2)
    piece = (2 * local_m, share // 2)
    return pl.pallas_call(
        functools.partial(reduce_kernel, n, pols),
        out_shape=shape((local_m, share), f32),
        in_specs=[vmem, vmem],
        out_specs=vmem,
        scratch_shapes=[
            pltpu.VMEM((pols // 2, n, local_m, share), f32),
            pltpu.VMEM((pols // 2, n) + piece, bf16),
            pltpu.VMEM((everyone - 1,) + piece, bf16),
            pltpu.VMEM((pols - 1, local_m, share), f32),
            sem((pols // 2,)), sem((pols // 2,)),
            sem((everyone - 1,)), sem((everyone - 1,)),
            sem((pols - 1,)), sem((pols - 1,)),
        ],
        compiler_params=pltpu.CompilerParams(
            collective_id=1, has_side_effects=True, vmem_limit_bytes=40 * 2**20
        ),
    )(prior, data)


def solution(mesh):
    placed = (P("ma", None), P("ma", "pol"), P("ma", "pol", None), P("ma"), P(), P())
    return jax.shard_map(
        shards, mesh=mesh, in_specs=placed, out_specs=P("ma", "pol"), check_vma=False
    )
```

```python
import functools
import math

import jax
import jax.numpy as jnp
from jax import lax
from jax.experimental import pallas as pl
from jax.experimental.pallas import tpu as pltpu
from jax.sharding import PartitionSpec as P

L = 2048
J = 8
CYCLES = 2 * L
FINE_ELL = 32
PIX_FINE = 128
PIX_TILE = 512
MESH = pl.DeviceIdType.MESH

smoothing = 0.1
prior_weight = 0.2


def short_waves(angle):
    z = angle * angle
    sine = angle * (1.0 + z * (-1.0 / 6 + z * (1.0 / 120 + z * (-1.0 / 5040 + z / 362880.0))))
    cosine = 1.0 + z * (
        -0.5 + z * (1.0 / 24 + z * (-1.0 / 720 + z * (1.0 / 40320 - z / 3628800.0)))
    )
    return cosine, sine


def turn(steps, period):
    centred = jnp.bitwise_and(steps, period - 1) - period // 2
    cosine, sine = short_waves(centred.astype(jnp.float32) * (0.5 * math.pi / period))
    cosine, sine = 1.0 - 2.0 * sine * sine, 2.0 * sine * cosine
    return 2.0 * sine * sine - 1.0, -2.0 * sine * cosine


def band_row(low, high):
    ell = lax.broadcasted_iota(jnp.int32, (1, L), 1)
    span = jnp.broadcast_to(high - low, (1, L)).astype(jnp.float32)
    fraction = (ell - low).astype(jnp.float32) / span
    inside = (ell >= low) & (ell <= high)
    cosine, sine = short_waves(0.5 * math.pi * (jnp.where(inside, fraction, 0.5) - 0.5))
    return jnp.where(inside, (1.0 - 2.0 * sine * sine) ** 2, 0.0)


def kernel(
    n, pols, sky_hbm, vis_hbm, limit_ref, order_ref, count_ref, beam_ref, out_ref,
    sky_ref, vis_ref, sky_rows, vis_rows, beam_buf, all_ref, data, data_in,
    tab, four, fort, coarse_cos, coarse_sin, kern, scaled, synth, total,
    prior_ref, mate_in, sums, peer_in,
    sky_sem, beam_sem, send1, recv1, send2, recv2, send_a, recv_a, send_b, recv_b, send_d, recv_d,
):
    ma = lax.axis_index("ma")
    pol = lax.axis_index("pol")
    side = lax.rem(pol, 2)
    mate = pol + 1 - 2 * side
    pairs = pols // 2
    pair = pol // 2
    everyone = n * pairs
    place = ma * pairs + pair
    local_m, modes, width = beam_buf.shape
    share = out_ref.shape[1]
    rows = four.shape[0]
    cycles = tab.shape[1]
    scales = synth.shape[0] // rows

    def beam_copy(i):
        return pltpu.make_async_copy(beam_ref.at[i], beam_buf.at[i], beam_sem.at[i])

    def sky_copy():
        return pltpu.make_async_copy(sky_hbm, sky_ref, sky_sem.at[0])

    def vis_copy():
        return pltpu.make_async_copy(vis_hbm, vis_ref, sky_sem.at[1])

    def sky_peer(d):
        return pltpu.make_async_remote_copy(
            src_ref=all_ref.at[side, ma], dst_ref=all_ref.at[side, ma],
            send_sem=send1.at[d], recv_sem=recv1.at[d],
            device_id=(lax.rem(ma + d, n), pol), device_id_type=MESH,
        )

    def sky_mate(d):
        source = lax.rem(ma + n - d, n)
        return pltpu.make_async_remote_copy(
            src_ref=all_ref.at[side, source], dst_ref=all_ref.at[side, source],
            send_sem=send2.at[d], recv_sem=recv2.at[d],
            device_id=(ma, mate), device_id_type=MESH,
        )

    def data_copy(d):
        other = lax.rem(pol + d, pols)
        return pltpu.make_async_remote_copy(
            src_ref=data.at[other], dst_ref=data_in.at[d - 1],
            send_sem=send_d.at[d - 1], recv_sem=recv_d.at[d - 1],
            device_id=(ma, other), device_id_type=MESH,
        )

    def mate_copy(h):
        return pltpu.make_async_remote_copy(
            src_ref=prior_ref.at[2 * h + 1 - side], dst_ref=mate_in.at[h],
            send_sem=send_a.at[h], recv_sem=recv_a.at[h],
            device_id=(ma, mate), device_id_type=MESH,
        )

    def peer_copy(d):
        target = lax.rem(place + d, everyone)
        target_ma = target // pairs
        target_pair = lax.rem(target, pairs)
        return pltpu.make_async_remote_copy(
            src_ref=sums.at[target_pair, target_ma], dst_ref=peer_in.at[d - 1],
            send_sem=send_b.at[d - 1], recv_sem=recv_b.at[d - 1],
            device_id=(target_ma, 2 * target_pair + side), device_id_type=MESH,
        )

    sky_copy().start()
    vis_copy().start()
    for i in range(local_m):
        beam_copy(i).start()

    barrier = pltpu.get_barrier_semaphore()

    @pl.loop(1, everyone)
    def _(d):
        target = lax.rem(place + d, everyone)
        pl.semaphore_signal(
            barrier, inc=1,
            device_id=(target // pairs, 2 * lax.rem(target, pairs) + side), device_id_type=MESH,
        )

    for d in range(1, pols, 2):
        pl.semaphore_signal(
            barrier, inc=1, device_id=(ma, lax.rem(pol + d, pols)), device_id_type=MESH
        )
    orders = jnp.zeros((local_m, 1), jnp.int32)
    for i in range(local_m):
        orders = jnp.where(
            lax.broadcasted_iota(jnp.int32, (local_m, 1), 0) == i, order_ref[ma * local_m + i], orders
        )
    sky_copy().wait()
    vis_copy().wait()
    alive = lax.rem(lax.broadcasted_iota(jnp.int32, (1, width), 1), L) >= orders
    masked = jnp.where(alive, sky_ref[...].astype(jnp.float32), 0.0)
    half = L // 2
    for h in range(2):
        all_ref[h, ma] = jnp.concatenate(
            [masked[:, h * half : (h + 1) * half], masked[:, L + h * half : L + (h + 1) * half]],
            axis=0,
        ).astype(jnp.bfloat16)
    vis = vis_ref[...].astype(jnp.float32)
    for i in range(local_m):
        sky_rows[i] = masked[i : i + 1]
        vis_rows[i] = vis[i : i + 1]

    pl.semaphore_wait(barrier, everyone - 1 + pairs)

    @pl.loop(1, n)
    def _(d):
        sky_peer(d).start()

    amplitude = math.sqrt(2.0 / L)
    norm = 1.0 / math.sqrt(rows // 2)

    def index(count, axis):
        return lax.broadcasted_iota(jnp.int32, (count, 1) if axis == 0 else (1, count), axis)

    table_rows = lax.broadcasted_iota(jnp.int32, (limit_ref.shape[0], 1), 0)
    for j in range(scales):
        low, high = [
            jnp.sum(
                jnp.where(table_rows == pol * scales + j, limit_ref[:, e : e + 1], 0),
                axis=0, keepdims=True,
            )
            for e in range(2)
        ]
        kern[j] = band_row(low, high)
    down_row, across_row = index(rows, 0), index(rows, 1)
    down_row = (down_row // (2 * local_m)) * local_m + lax.rem(down_row, local_m)
    across_row = (across_row // (2 * local_m)) * local_m + lax.rem(across_row, local_m)

    def place_order(i, found):
        order = order_ref[i]
        return (
            jnp.where(down_row == i, order, found[0]),
            jnp.where(across_row == i, order, found[1]),
        )

    down, across = lax.fori_loop(
        0, n * local_m, place_order, (jnp.zeros_like(down_row), jnp.zeros_like(across_row))
    )
    quarter = jnp.bitwise_and(down, 3)
    cp = jnp.where(quarter == 0, 1.0, jnp.where(quarter == 2, -1.0, 0.0))
    sp = jnp.where(quarter == 1, 1.0, jnp.where(quarter == 3, -1.0, 0.0))
    odd = 2 * (ma * cycles + index(cycles, 1)) + 1
    _, weight = turn(odd, 4 * CYCLES)

    period = 8 * CYCLES
    blocks = L // FINE_ELL
    coarse = 2 * FINE_ELL * index(blocks, 0) * odd - CYCLES
    for part in range(2):
        cosine, sine = turn(coarse - part * (period // 4), period)
        for b in range(blocks):
            coarse_cos[part * blocks + b] = amplitude * cosine[b : b + 1]
            coarse_sin[part * blocks + b] = amplitude * sine[b : b + 1]
    fine_cos, fine_sin = turn((2 * index(FINE_ELL, 0) + 1) * odd, period)

    @pl.loop(0, 2 * blocks)
    def _(b):
        at = pl.ds(pl.multiple_of(b * FINE_ELL, FINE_ELL), FINE_ELL)
        tab[at, :] = (fine_cos * coarse_cos[b] - fine_sin * coarse_sin[b]).astype(jnp.bfloat16)

    steps = CYCLES // PIX_FINE
    quarter_turn = CYCLES // 4
    down_part = lax.rem(index(rows, 0) // local_m, 2) * quarter_turn
    across_part = lax.rem(index(rows, 1) // local_m, 2) * quarter_turn
    down_fine = turn(down * index(PIX_FINE, 1), CYCLES)
    down_coarse = turn(down * (PIX_FINE * index(steps, 1)) + down_part, CYCLES)
    across_fine = turn(across * index(PIX_FINE, 0), CYCLES)
    across_coarse = turn(across * (PIX_FINE * index(steps, 0)) + across_part, CYCLES)
    down_fine = [norm * part for part in down_fine]
    across_fine = [norm * part for part in across_fine]
    for b in range(steps):
        at = slice(b * PIX_FINE, (b + 1) * PIX_FINE)
        four[:, at] = (
            down_fine[0] * down_coarse[0][:, b : b + 1]
            - down_fine[1] * down_coarse[1][:, b : b + 1]
        ).astype(jnp.bfloat16)
        fort[at, :] = (
            across_fine[0] * across_coarse[0][b : b + 1, :]
            - across_fine[1] * across_coarse[1][b : b + 1, :]
        ).astype(jnp.bfloat16)

    mode_index = pol * modes + lax.broadcasted_iota(jnp.int32, (modes, 1), 0)
    diagonal = lax.broadcasted_iota(jnp.int32, (modes, modes), 0) == lax.broadcasted_iota(
        jnp.int32, (modes, modes), 1
    )

    def one_order(i):
        beam_copy(i).wait()
        mine = lax.broadcasted_iota(jnp.int32, (local_m, 1), 0) == i
        total = jnp.where(diagonal, -vis_rows[i], 0.0)
        for t in range(0, width, 128):
            row = sky_rows[i, :, t : t + 128]
            total = total + beam_buf[i, :, t : t + 128].astype(jnp.float32) * row
        image = jnp.sum(total, axis=1, keepdims=True)
        misfit = jnp.where(mode_index < count_ref[i], image, 0.0)
        spread = jnp.broadcast_to(
            misfit.astype(jnp.bfloat16).astype(jnp.float32), (modes, 128)
        )
        for t in range(0, width, 128):
            column = jnp.sum(
                beam_buf[i, :, t : t + 128].astype(jnp.float32) * spread, axis=0, keepdims=True
            )
            b, o = t // share, t % share
            data[b, :, o : o + 128] += jnp.where(mine, column, 0.0)

    data[...] = jnp.zeros_like(data)

    @pl.loop(1, n)
    def _(d):
        sky_peer(d).wait_recv()
        sky_mate(d).start()

    @pl.loop(0, local_m)
    def _(i):
        one_order(i)

    for b in range(pols):
        ell = lax.rem(b * share + lax.broadcasted_iota(jnp.int32, (1, share), 1), L)
        data[b] = jnp.where(ell >= orders, data[b], 0.0)
    for d in range(1, pols):
        data_copy(d).start()

    @pl.loop(1, n)
    def _(d):
        sky_mate(d).wait_recv()

    for j in range(scales):
        for h in range(2):
            for d in range(n):
                scaled[2 * local_m * d : 2 * local_m * (d + 1), h * half : (h + 1) * half] = (
                    kern[j, :, h * half : (h + 1) * half] * all_ref[h, d].astype(jnp.float32)
                ).astype(jnp.bfloat16)
        with_cos = jnp.dot(scaled[...], tab[0:L, :], preferred_element_type=jnp.float32)
        with_sin = jnp.dot(scaled[...], tab[L : 2 * L, :], preferred_element_type=jnp.float32)
        synth[j * rows : (j + 1) * rows, :] = (cp * with_cos - sp * with_sin).astype(jnp.bfloat16)

    total[...] = jnp.zeros_like(total)

    @pl.loop(0, CYCLES // PIX_TILE)
    def _(t):
        at = pl.ds(pl.multiple_of(t * PIX_TILE, PIX_TILE), PIX_TILE)
        left = fort[at, :]
        right = four[:, at]
        for j in range(scales):
            mine = slice(j * rows, (j + 1) * rows)
            pixels = jnp.dot(left, synth[mine, :], preferred_element_type=jnp.float32)
            slopes = (
                weight * pixels * lax.rsqrt(pixels * pixels + smoothing * smoothing)
            ).astype(jnp.bfloat16)
            total[mine, :] += jnp.dot(right, slopes, preferred_element_type=jnp.float32)

    contract_last = (((1,), (1,)), ((), ()))

    def back(block):
        t = pl.multiple_of(block * share, share)
        ell = t + lax.broadcasted_iota(jnp.int32, (1, share), 1)
        prior = jnp.zeros((rows, share), jnp.float32)
        for j in range(scales):
            cycle_b = total[j * rows : (j + 1) * rows, :].astype(jnp.bfloat16)
            back_cos = lax.dot_general(
                cycle_b, tab[pl.ds(t, share), :], contract_last,
                preferred_element_type=jnp.float32,
            )
            back_sin = lax.dot_general(
                cycle_b, tab[pl.ds(L + t, share), :], contract_last,
                preferred_element_type=jnp.float32,
            )
            prior = prior + kern[j, :, pl.ds(t, share)] * (cp * back_cos - sp * back_sin)
        prior = jnp.where(ell >= down, prior_weight * prior, 0.0)
        for d in range(n):
            for c in range(2):
                first = (2 * d + c) * local_m
                prior_ref[c * pairs + block, d] = prior[first : first + local_m, :]

    for b in range(0, pairs, 2):
        back(b + 1 - side)
    for h in range(pairs):
        mate_copy(h).start()
    for b in range(0, pairs, 2):
        back(b + side)
    for h in range(pairs):
        mate_copy(h).wait_recv()
        both = prior_ref[2 * h + side] + mate_in[h]
        sums[h] = jnp.concatenate(
            [both[:, :, : share // 2], both[:, :, share // 2 :]], axis=1
        ).astype(jnp.bfloat16)

    @pl.loop(1, everyone)
    def _(d):
        peer_copy(d).start()

    result = data[pol] + (prior_ref[pol, ma] + mate_in[pair, ma])
    for d in range(1, pols):
        data_copy(d).wait_recv()
        result = result + data_in[d - 1]

    def add(d, running):
        peer_copy(d).wait_recv()
        return running + peer_in[d - 1].astype(jnp.float32)

    prior = lax.fori_loop(1, everyone, add, jnp.zeros(peer_in.shape[1:], jnp.float32))
    out_ref[:, : share // 2] = result[:, : share // 2] + prior[:local_m]
    out_ref[:, share // 2 :] = result[:, share // 2 :] + prior[local_m:]

    for h in range(pairs):
        mate_copy(h).wait_send()
    for d in range(1, pols):
        data_copy(d).wait_send()

    @pl.loop(1, everyone)
    def _(d):
        peer_copy(d).wait_send()

    @pl.loop(1, n)
    def _(d):
        sky_peer(d).wait_send()
        sky_mate(d).wait_send()


def shards(sky_coeffs, visibilities, beam_blocks, mode_counts, order_table, band_limits):
    local_m, width = sky_coeffs.shape
    modes = beam_blocks.shape[1]
    n = lax.axis_size("ma")
    pols = lax.axis_size("pol")
    cycles = CYCLES // n
    scales = J // pols
    share = width // pols
    pairs = pols // 2
    everyone = n * pairs
    rows = 2 * n * local_m
    piece = (2 * local_m, share // 2)
    vmem = pl.BlockSpec(memory_space=pltpu.VMEM)
    smem = pl.BlockSpec(memory_space=pltpu.SMEM)
    hbm = pl.BlockSpec(memory_space=pl.ANY)
    f32, bf16 = jnp.float32, jnp.bfloat16
    sem = pltpu.SemaphoreType.DMA
    return pl.pallas_call(
        functools.partial(kernel, n, pols),
        out_shape=jax.ShapeDtypeStruct((local_m, share), f32),
        in_specs=[hbm, hbm, vmem, smem, smem, hbm],
        out_specs=vmem,
        scratch_shapes=[
            pltpu.VMEM((local_m, width), bf16),
            pltpu.VMEM((local_m, modes), bf16),
            pltpu.VMEM((local_m, 1, width), f32),
            pltpu.VMEM((local_m, 1, modes), f32),
            pltpu.VMEM((local_m, modes, width), bf16),
            pltpu.VMEM((2, n, 2 * local_m, L // 2), bf16),
            pltpu.VMEM((pols, local_m, share), f32),
            pltpu.VMEM((pols - 1, local_m, share), f32),
            pltpu.VMEM((2 * L, cycles), bf16),
            pltpu.VMEM((rows, CYCLES), bf16),
            pltpu.VMEM((CYCLES, rows), bf16),
            pltpu.VMEM((2 * L // FINE_ELL, 1, cycles), f32),
            pltpu.VMEM((2 * L // FINE_ELL, 1, cycles), f32),
            pltpu.VMEM((scales, 1, L), f32),
            pltpu.VMEM((rows, L), bf16),
            pltpu.VMEM((scales * rows, cycles), bf16),
            pltpu.VMEM((scales * rows, cycles), f32),
            pltpu.VMEM((pols, n, local_m, share), f32),
            pltpu.VMEM((pairs, n, local_m, share), f32),
            pltpu.VMEM((pairs, n) + piece, bf16),
            pltpu.VMEM((everyone - 1,) + piece, bf16),
            sem((2,)), sem((local_m,)),
            sem((n,)), sem((n,)), sem((n,)), sem((n,)),
            sem((pairs,)), sem((pairs,)),
            sem((everyone - 1,)), sem((everyone - 1,)),
            sem((pols - 1,)), sem((pols - 1,)),
        ],
        compiler_params=pltpu.CompilerParams(
            collective_id=0, has_side_effects=True, vmem_limit_bytes=60 * 2**20
        ),
    )(sky_coeffs, visibilities, band_limits, order_table, mode_counts, beam_blocks)


def solution(mesh):
    placed = (P("ma", None), P("ma", "pol"), P("ma", "pol", None), P("ma"), P(), P())
    return jax.shard_map(
        shards, mesh=mesh, in_specs=placed, out_specs=P("ma", "pol"), check_vma=False
    )
```

```python
import functools
import math

import jax
import jax.numpy as jnp
from jax import lax
from jax.experimental import pallas as pl
from jax.experimental.pallas import tpu as pltpu
from jax.sharding import PartitionSpec as P

L = 2048
J = 8
CYCLES = 2 * L
FINE_ELL = 32
PIX_FINE = 128
PIX_TILE = 512
MESH = pl.DeviceIdType.MESH

smoothing = 0.1
prior_weight = 0.2


def short_waves(angle):
    z = angle * angle
    sine = angle * (1.0 + z * (-1.0 / 6 + z * (1.0 / 120 + z * (-1.0 / 5040 + z / 362880.0))))
    cosine = 1.0 + z * (
        -0.5 + z * (1.0 / 24 + z * (-1.0 / 720 + z * (1.0 / 40320 - z / 3628800.0)))
    )
    return cosine, sine


def turn(steps, period):
    centred = jnp.bitwise_and(steps, period - 1) - period // 2
    cosine, sine = short_waves(centred.astype(jnp.float32) * (0.5 * math.pi / period))
    cosine, sine = 1.0 - 2.0 * sine * sine, 2.0 * sine * cosine
    return 2.0 * sine * sine - 1.0, -2.0 * sine * cosine


def band_row(low, high):
    ell = lax.broadcasted_iota(jnp.int32, (1, L), 1)
    span = jnp.broadcast_to(high - low, (1, L)).astype(jnp.float32)
    fraction = (ell - low).astype(jnp.float32) / span
    inside = (ell >= low) & (ell <= high)
    cosine, sine = short_waves(0.5 * math.pi * (jnp.where(inside, fraction, 0.5) - 0.5))
    return jnp.where(inside, (1.0 - 2.0 * sine * sine) ** 2, 0.0)


def kernel(
    n, pols, sky_hbm, vis_hbm, limit_ref, order_ref, count_ref, beam_ref, out_ref,
    sky_ref, vis_ref, sky_rows, vis_rows, beam_buf, all_ref, data, data_in,
    tab, four, fort, coarse_cos, coarse_sin, kern, scaled, synth, total,
    prior_ref, mate_in, sums, peer_in,
    sky_sem, beam_sem, send1, recv1, send2, recv2, send_a, recv_a, send_b, recv_b, send_d, recv_d,
):
    ma = lax.axis_index("ma")
    pol = lax.axis_index("pol")
    side = lax.rem(pol, 2)
    mate = pol + 1 - 2 * side
    pairs = pols // 2
    pair = pol // 2
    everyone = n * pairs
    place = ma * pairs + pair
    local_m, modes, width = beam_buf.shape
    share = out_ref.shape[1]
    rows = four.shape[0]
    cycles = tab.shape[1]
    scales = synth.shape[0] // rows

    def beam_copy(i):
        return pltpu.make_async_copy(beam_ref.at[i], beam_buf.at[i], beam_sem.at[i])

    def sky_copy():
        return pltpu.make_async_copy(sky_hbm, sky_ref, sky_sem.at[0])

    def vis_copy():
        return pltpu.make_async_copy(vis_hbm, vis_ref, sky_sem.at[1])

    def sky_peer(d):
        return pltpu.make_async_remote_copy(
            src_ref=all_ref.at[side, ma], dst_ref=all_ref.at[side, ma],
            send_sem=send1.at[d], recv_sem=recv1.at[d],
            device_id=(lax.rem(ma + d, n), pol), device_id_type=MESH,
        )

    def sky_mate(d):
        source = lax.rem(ma + n - d, n)
        return pltpu.make_async_remote_copy(
            src_ref=all_ref.at[side, source], dst_ref=all_ref.at[side, source],
            send_sem=send2.at[d], recv_sem=recv2.at[d],
            device_id=(ma, mate), device_id_type=MESH,
        )

    def data_copy(d):
        other = lax.rem(pol + d, pols)
        return pltpu.make_async_remote_copy(
            src_ref=data.at[other], dst_ref=data_in.at[d - 1],
            send_sem=send_d.at[d - 1], recv_sem=recv_d.at[d - 1],
            device_id=(ma, other), device_id_type=MESH,
        )

    def mate_copy(h):
        return pltpu.make_async_remote_copy(
            src_ref=prior_ref.at[2 * h + 1 - side], dst_ref=mate_in.at[h],
            send_sem=send_a.at[h], recv_sem=recv_a.at[h],
            device_id=(ma, mate), device_id_type=MESH,
        )

    def peer_copy(d):
        target = lax.rem(place + d, everyone)
        target_ma = target // pairs
        target_pair = lax.rem(target, pairs)
        return pltpu.make_async_remote_copy(
            src_ref=sums.at[target_pair, target_ma], dst_ref=peer_in.at[d - 1],
            send_sem=send_b.at[d - 1], recv_sem=recv_b.at[d - 1],
            device_id=(target_ma, 2 * target_pair + side), device_id_type=MESH,
        )

    sky_copy().start()
    vis_copy().start()
    for i in range(local_m):
        beam_copy(i).start()

    barrier = pltpu.get_barrier_semaphore()

    @pl.loop(1, everyone)
    def _(d):
        target = lax.rem(place + d, everyone)
        pl.semaphore_signal(
            barrier, inc=1,
            device_id=(target // pairs, 2 * lax.rem(target, pairs) + side), device_id_type=MESH,
        )

    for d in range(1, pols, 2):
        pl.semaphore_signal(
            barrier, inc=1, device_id=(ma, lax.rem(pol + d, pols)), device_id_type=MESH
        )
    orders = jnp.zeros((local_m, 1), jnp.int32)
    for i in range(local_m):
        orders = jnp.where(
            lax.broadcasted_iota(jnp.int32, (local_m, 1), 0) == i, order_ref[ma * local_m + i], orders
        )
    sky_copy().wait()
    vis_copy().wait()
    alive = lax.rem(lax.broadcasted_iota(jnp.int32, (1, width), 1), L) >= orders
    masked = jnp.where(alive, sky_ref[...].astype(jnp.float32), 0.0)
    half = L // 2
    for h in range(2):
        all_ref[h, ma] = jnp.concatenate(
            [masked[:, h * half : (h + 1) * half], masked[:, L + h * half : L + (h + 1) * half]],
            axis=0,
        ).astype(jnp.bfloat16)
    vis = vis_ref[...].astype(jnp.float32)
    for i in range(local_m):
        sky_rows[i] = masked[i : i + 1]
        vis_rows[i] = vis[i : i + 1]

    pl.semaphore_wait(barrier, everyone - 1 + pairs)

    @pl.loop(1, n)
    def _(d):
        sky_peer(d).start()

    amplitude = math.sqrt(2.0 / L)
    norm = 1.0 / math.sqrt(rows // 2)

    def index(count, axis):
        return lax.broadcasted_iota(jnp.int32, (count, 1) if axis == 0 else (1, count), axis)

    table_columns = lax.broadcasted_iota(jnp.int32, (1, limit_ref.shape[1]), 1)
    for j in range(scales):
        low, high = [
            jnp.sum(
                jnp.where(
                    table_columns == pol * scales + j,
                    limit_ref[e : e + 1, :].astype(jnp.float32), 0.0,
                ),
                axis=1, keepdims=True,
            ).astype(jnp.int32)
            for e in range(2)
        ]
        kern[j] = band_row(low, high)
    down_row, across_row = index(rows, 0), index(rows, 1)
    down_row = (down_row // (2 * local_m)) * local_m + lax.rem(down_row, local_m)
    across_row = (across_row // (2 * local_m)) * local_m + lax.rem(across_row, local_m)

    def place_order(i, found):
        order = order_ref[i]
        return (
            jnp.where(down_row == i, order, found[0]),
            jnp.where(across_row == i, order, found[1]),
        )

    down, across = lax.fori_loop(
        0, n * local_m, place_order, (jnp.zeros_like(down_row), jnp.zeros_like(across_row))
    )
    quarter = jnp.bitwise_and(down, 3)
    cp = jnp.where(quarter == 0, 1.0, jnp.where(quarter == 2, -1.0, 0.0))
    sp = jnp.where(quarter == 1, 1.0, jnp.where(quarter == 3, -1.0, 0.0))
    odd = 2 * (ma * cycles + index(cycles, 1)) + 1
    _, weight = turn(odd, 4 * CYCLES)

    period = 8 * CYCLES
    blocks = L // FINE_ELL
    coarse = 2 * FINE_ELL * index(blocks, 0) * odd - CYCLES
    for part in range(2):
        cosine, sine = turn(coarse - part * (period // 4), period)
        for b in range(blocks):
            coarse_cos[part * blocks + b] = amplitude * cosine[b : b + 1]
            coarse_sin[part * blocks + b] = amplitude * sine[b : b + 1]
    fine_cos, fine_sin = turn((2 * index(FINE_ELL, 0) + 1) * odd, period)

    @pl.loop(0, 2 * blocks)
    def _(b):
        at = pl.ds(pl.multiple_of(b * FINE_ELL, FINE_ELL), FINE_ELL)
        tab[at, :] = (fine_cos * coarse_cos[b] - fine_sin * coarse_sin[b]).astype(jnp.bfloat16)

    steps = CYCLES // PIX_FINE
    quarter_turn = CYCLES // 4
    down_part = lax.rem(index(rows, 0) // local_m, 2) * quarter_turn
    across_part = lax.rem(index(rows, 1) // local_m, 2) * quarter_turn
    down_fine = turn(down * index(PIX_FINE, 1), CYCLES)
    down_coarse = turn(down * (PIX_FINE * index(steps, 1)) + down_part, CYCLES)
    across_fine = turn(across * index(PIX_FINE, 0), CYCLES)
    across_coarse = turn(across * (PIX_FINE * index(steps, 0)) + across_part, CYCLES)
    down_fine = [norm * part for part in down_fine]
    across_fine = [norm * part for part in across_fine]
    for b in range(steps):
        at = slice(b * PIX_FINE, (b + 1) * PIX_FINE)
        four[:, at] = (
            down_fine[0] * down_coarse[0][:, b : b + 1]
            - down_fine[1] * down_coarse[1][:, b : b + 1]
        ).astype(jnp.bfloat16)
        fort[at, :] = (
            across_fine[0] * across_coarse[0][b : b + 1, :]
            - across_fine[1] * across_coarse[1][b : b + 1, :]
        ).astype(jnp.bfloat16)

    mode_index = pol * modes + lax.broadcasted_iota(jnp.int32, (modes, 1), 0)
    diagonal = lax.broadcasted_iota(jnp.int32, (modes, modes), 0) == lax.broadcasted_iota(
        jnp.int32, (modes, modes), 1
    )

    def one_order(i):
        beam_copy(i).wait()
        mine = lax.broadcasted_iota(jnp.int32, (local_m, 1), 0) == i
        total = jnp.where(diagonal, -vis_rows[i], 0.0)
        for t in range(0, width, 128):
            row = sky_rows[i, :, t : t + 128]
            total = total + beam_buf[i, :, t : t + 128].astype(jnp.float32) * row
        image = jnp.sum(total, axis=1, keepdims=True)
        misfit = jnp.where(mode_index < count_ref[i], image, 0.0)
        spread = jnp.broadcast_to(
            misfit.astype(jnp.bfloat16).astype(jnp.float32), (modes, 128)
        )
        for t in range(0, width, 128):
            column = jnp.sum(
                beam_buf[i, :, t : t + 128].astype(jnp.float32) * spread, axis=0, keepdims=True
            )
            b, o = t // share, t % share
            data[b, :, o : o + 128] += jnp.where(mine, column, 0.0)

    data[...] = jnp.zeros_like(data)
    early = local_m // 2

    @pl.loop(0, early)
    def _(i):
        one_order(i)

    @pl.loop(1, n)
    def _(d):
        sky_peer(d).wait_recv()
        sky_mate(d).start()

    @pl.loop(early, local_m)
    def _(i):
        one_order(i)

    for b in range(pols):
        ell = lax.rem(b * share + lax.broadcasted_iota(jnp.int32, (1, share), 1), L)
        data[b] = jnp.where(ell >= orders, data[b], 0.0)
    for d in range(1, pols):
        data_copy(d).start()

    @pl.loop(1, n)
    def _(d):
        sky_mate(d).wait_recv()

    for j in range(scales):
        for h in range(2):
            for d in range(n):
                scaled[2 * local_m * d : 2 * local_m * (d + 1), h * half : (h + 1) * half] = (
                    kern[j, :, h * half : (h + 1) * half] * all_ref[h, d].astype(jnp.float32)
                ).astype(jnp.bfloat16)
        with_cos = jnp.dot(scaled[...], tab[0:L, :], preferred_element_type=jnp.float32)
        with_sin = jnp.dot(scaled[...], tab[L : 2 * L, :], preferred_element_type=jnp.float32)
        synth[j * rows : (j + 1) * rows, :] = (cp * with_cos - sp * with_sin).astype(jnp.bfloat16)

    total[...] = jnp.zeros_like(total)

    @pl.loop(0, CYCLES // PIX_TILE)
    def _(t):
        at = pl.ds(pl.multiple_of(t * PIX_TILE, PIX_TILE), PIX_TILE)
        left = fort[at, :]
        right = four[:, at]
        for j in range(scales):
            mine = slice(j * rows, (j + 1) * rows)
            pixels = jnp.dot(left, synth[mine, :], preferred_element_type=jnp.float32)
            slopes = (
                weight * pixels * lax.rsqrt(pixels * pixels + smoothing * smoothing)
            ).astype(jnp.bfloat16)
            total[mine, :] += jnp.dot(right, slopes, preferred_element_type=jnp.float32)

    contract_last = (((1,), (1,)), ((), ()))

    def back(block):
        t = pl.multiple_of(block * share, share)
        ell = t + lax.broadcasted_iota(jnp.int32, (1, share), 1)
        prior = jnp.zeros((rows, share), jnp.float32)
        for j in range(scales):
            cycle_b = total[j * rows : (j + 1) * rows, :].astype(jnp.bfloat16)
            back_cos = lax.dot_general(
                cycle_b, tab[pl.ds(t, share), :], contract_last,
                preferred_element_type=jnp.float32,
            )
            back_sin = lax.dot_general(
                cycle_b, tab[pl.ds(L + t, share), :], contract_last,
                preferred_element_type=jnp.float32,
            )
            prior = prior + kern[j, :, pl.ds(t, share)] * (cp * back_cos - sp * back_sin)
        prior = jnp.where(ell >= down, prior_weight * prior, 0.0)
        for d in range(n):
            for c in range(2):
                first = (2 * d + c) * local_m
                prior_ref[c * pairs + block, d] = prior[first : first + local_m, :]

    for b in range(0, pairs, 2):
        back(b + 1 - side)
    for h in range(pairs):
        mate_copy(h).start()
    for b in range(0, pairs, 2):
        back(b + side)
    for h in range(pairs):
        mate_copy(h).wait_recv()
        both = prior_ref[2 * h + side] + mate_in[h]
        sums[h] = jnp.concatenate(
            [both[:, :, : share // 2], both[:, :, share // 2 :]], axis=1
        ).astype(jnp.bfloat16)

    @pl.loop(1, everyone)
    def _(d):
        peer_copy(d).start()

    result = data[pol] + (prior_ref[pol, ma] + mate_in[pair, ma])
    for d in range(1, pols):
        data_copy(d).wait_recv()
        result = result + data_in[d - 1]

    def add(d, running):
        peer_copy(d).wait_recv()
        return running + peer_in[d - 1].astype(jnp.float32)

    prior = lax.fori_loop(1, everyone, add, jnp.zeros(peer_in.shape[1:], jnp.float32))
    out_ref[:, : share // 2] = result[:, : share // 2] + prior[:local_m]
    out_ref[:, share // 2 :] = result[:, share // 2 :] + prior[local_m:]

    for h in range(pairs):
        mate_copy(h).wait_send()
    for d in range(1, pols):
        data_copy(d).wait_send()

    @pl.loop(1, everyone)
    def _(d):
        peer_copy(d).wait_send()

    @pl.loop(1, n)
    def _(d):
        sky_peer(d).wait_send()
        sky_mate(d).wait_send()


def shards(sky_coeffs, visibilities, beam_blocks, mode_counts, order_table, band_limits):
    local_m, width = sky_coeffs.shape
    modes = beam_blocks.shape[1]
    n = lax.axis_size("ma")
    pols = lax.axis_size("pol")
    cycles = CYCLES // n
    scales = J // pols
    share = width // pols
    pairs = pols // 2
    everyone = n * pairs
    rows = 2 * n * local_m
    piece = (2 * local_m, share // 2)
    vmem = pl.BlockSpec(memory_space=pltpu.VMEM)
    smem = pl.BlockSpec(memory_space=pltpu.SMEM)
    hbm = pl.BlockSpec(memory_space=pl.ANY)
    f32, bf16 = jnp.float32, jnp.bfloat16
    sem = pltpu.SemaphoreType.DMA
    return pl.pallas_call(
        functools.partial(kernel, n, pols),
        out_shape=jax.ShapeDtypeStruct((local_m, share), f32),
        in_specs=[hbm, hbm, vmem, smem, smem, hbm],
        out_specs=vmem,
        scratch_shapes=[
            pltpu.VMEM((local_m, width), bf16),
            pltpu.VMEM((local_m, modes), bf16),
            pltpu.VMEM((local_m, 1, width), f32),
            pltpu.VMEM((local_m, 1, modes), f32),
            pltpu.VMEM((local_m, modes, width), bf16),
            pltpu.VMEM((2, n, 2 * local_m, L // 2), bf16),
            pltpu.VMEM((pols, local_m, share), f32),
            pltpu.VMEM((pols - 1, local_m, share), f32),
            pltpu.VMEM((2 * L, cycles), bf16),
            pltpu.VMEM((rows, CYCLES), bf16),
            pltpu.VMEM((CYCLES, rows), bf16),
            pltpu.VMEM((2 * L // FINE_ELL, 1, cycles), f32),
            pltpu.VMEM((2 * L // FINE_ELL, 1, cycles), f32),
            pltpu.VMEM((scales, 1, L), f32),
            pltpu.VMEM((rows, L), bf16),
            pltpu.VMEM((scales * rows, cycles), bf16),
            pltpu.VMEM((scales * rows, cycles), f32),
            pltpu.VMEM((pols, n, local_m, share), f32),
            pltpu.VMEM((pairs, n, local_m, share), f32),
            pltpu.VMEM((pairs, n) + piece, bf16),
            pltpu.VMEM((everyone - 1,) + piece, bf16),
            sem((2,)), sem((local_m,)),
            sem((n,)), sem((n,)), sem((n,)), sem((n,)),
            sem((pairs,)), sem((pairs,)),
            sem((everyone - 1,)), sem((everyone - 1,)),
            sem((pols - 1,)), sem((pols - 1,)),
        ],
        compiler_params=pltpu.CompilerParams(
            collective_id=0, has_side_effects=True, vmem_limit_bytes=60 * 2**20
        ),
    )(sky_coeffs, visibilities, band_limits.T, order_table, mode_counts, beam_blocks)


def solution(mesh):
    placed = (P("ma", None), P("ma", "pol"), P("ma", "pol", None), P("ma"), P(), P())
    return jax.shard_map(
        shards, mesh=mesh, in_specs=placed, out_specs=P("ma", "pol"), check_vma=False
    )
```
